512 devices in a mesh: ed: 64 (over z, x_hi, core), tp: 8 (over y, x_lo).
Axes of the slice: x: 4 (x_hi: 2, x_lo: 2; x = x_hi * 2 + x_lo), y: 4, z: 16, core: 2. Of those that a mesh axis runs over, the one named last changes fastest.
Arguments:
- tokens: bfloat16 [8192, 3072], P('ed', 'tp'), may hold values from -6 to 6
- gate_weight: bfloat16 [64, 3072, 2048], P('ed', None, 'tp'), as said below
- up_weight: bfloat16 [64, 3072, 2048], P('ed', None, 'tp'), as said below
- experts: int32 [8192, 2], P('ed'), may hold values from 0 to 7, as said below
- placement: int32 [16], replicated, may hold values from 0 to 7, as said below
- mix_weight: float32 [8192, 2], P('ed'), may hold values from 0.1 to 1
Outputs:
- expert_out: bfloat16 [8192, 2, 8192], P('ed', None, 'tp')
The draws below stay inside these ranges and needn't reach their ends.
Inputs may be any that keep to these rules, and one draw needn't show every extreme that they name: Each token names two different experts. In each aligned block of 128 tokens, at most 32 times the number of slots holding e of the block's choices name expert e, and some expert held by one slot is named exactly 32 times. `placement`: never falls; every expert is held by 1 to 6 slots. `gate_weight`: rows s * 4 + g and r * 4 + g are equal whenever placement[s] = placement[r]. `up_weight`: rows s * 4 + g and r * 4 + g are equal whenever placement[s] = placement[r].
All inputs are finite; a program needn't handle non-finite values.
Results may differ from the reference program's by a relative error of at most 0.0049.
Values may be sent and summed in bfloat16 or wider, within the bound.
A program may use at most 64 MiB of HBM per device.

```python
import jax
import jax.numpy as jnp
from jax import lax

D = 3072
FF = 8192
EXPERTS = 8
TOP = 2
SLOTS = 16
TOK_DEV = 128
MOST = 32
GROUP = 4
FFG = 2048
FF_DEV = 256
TOKENS = 8192
N_ED = 64
N_TP = 8


def slot_table(key):
    ranking = jax.random.permutation(key, EXPERTS)
    per_rank = jnp.array([6, 3, 2, 1, 1, 1, 1, 1], dtype=jnp.int32)
    per_expert = jnp.zeros((EXPERTS,), jnp.int32).at[ranking].set(per_rank)
    bounds = jnp.cumsum(per_expert)
    slot_range = jnp.arange(SLOTS, dtype=jnp.int32)
    placement_list = jnp.sum((slot_range[:, None] >= bounds[None, :]).astype(jnp.int32), axis=1)
    return (ranking, placement_list)


def spread_slots(expert_part, placement_list):
    return expert_part[placement_list].reshape(SLOTS * GROUP, D, FFG)


def draw_placement(key, part):
    ranking, placement_list = slot_table(key)
    return placement_list.astype(jnp.int32)


def shuffle_one(sub_key):
    return jax.random.permutation(sub_key, TOK_DEV)


def draw_experts(key, part):
    ranking, placement_list = slot_table(key)
    key = jax.random.fold_in(key, 5)
    device_count = TOKENS // TOK_DEV
    most_rows = TOK_DEV // 4
    split_keys = jax.random.split(key, 6)
    extra_first = jax.random.randint(split_keys[0], (device_count,), 0, most_rows // 2 + 1)
    extra_second = jax.random.randint(split_keys[1], (device_count,), 0, most_rows // 2 + 1)
    extra_third = jax.random.randint(split_keys[2], (device_count,), 0, most_rows)
    extra_fourth = jax.random.randint(split_keys[3], (device_count,), 0, most_rows // 2 + 1)
    per_rank = jnp.stack([most_rows + extra_first + extra_second, most_rows + extra_third + extra_fourth, most_rows - extra_third, most_rows + 0 * extra_first, most_rows - extra_first, most_rows - extra_second, most_rows - extra_fourth, most_rows + 0 * extra_first], axis=1)
    per_expert = jnp.zeros((device_count, EXPERTS), jnp.int32).at[:, ranking].set(per_rank.astype(jnp.int32))
    bounds = jnp.cumsum(per_expert, axis=1)
    pair_range = jnp.arange(2 * TOK_DEV, dtype=jnp.int32)
    labels = jnp.sum((pair_range[None, :, None] >= bounds[:, None, :]).astype(jnp.int32), axis=2)
    first_half = labels[:, :TOK_DEV]
    second_half = labels[:, TOK_DEV:]
    flip_order = jax.random.randint(split_keys[4], (device_count, TOK_DEV), 0, 2)
    leading = jnp.where(flip_order == 1, second_half, first_half)
    trailing = jnp.where(flip_order == 1, first_half, second_half)
    shuffles = jax.vmap(shuffle_one)(jax.random.split(split_keys[5], device_count))
    leading = jnp.take_along_axis(leading, shuffles, axis=1)
    trailing = jnp.take_along_axis(trailing, shuffles, axis=1)
    return jnp.stack([leading, trailing], axis=2).reshape(TOKENS, TOP).astype(jnp.int32)


def draw_gate_weight(key, part):
    ranking, placement_list = slot_table(key)
    key = jax.random.fold_in(key, 7)
    expert_part = jax.random.normal(key, (EXPERTS, GROUP, D, FFG), jnp.float32)
    return spread_slots((expert_part * D ** (-0.5)).astype(jnp.bfloat16), placement_list)


def draw_up_weight(key, part):
    ranking, placement_list = slot_table(key)
    key = jax.random.fold_in(key, 11)
    expert_part = jax.random.normal(key, (EXPERTS, GROUP, D, FFG), jnp.float32)
    return spread_slots((expert_part * D ** (-0.5)).astype(jnp.bfloat16), placement_list)


def level_of(stream_key, extent, cuts, smallest, high):
    factor_of = 1.0
    for dim, shards_of in cuts:
        draws = jax.random.uniform(jax.random.fold_in(jax.random.fold_in(stream_key, 6), dim), (shards_of,), jnp.float32, smallest / len(cuts), high / len(cuts))
        factor_of = factor_of * jnp.repeat(jnp.exp(draws), extent[dim] // shards_of).reshape((-1,) + (1,) * (len(extent) - 1 - dim))
    return factor_of


def normal_values(key, shape, width, reach, cuts=(), kind=jnp.bfloat16):
    level = level_of(key, shape, cuts, -0.22, 0.18) if cuts else 1.0
    drawn = jax.random.normal(key, shape, jnp.float32) * width * level
    return jnp.minimum(jnp.maximum(drawn, -reach), reach).astype(kind)


def setup_inputs(seed: int = 0) -> dict:
    splits = jax.random.split(jax.random.key(seed), 7)
    tokens = normal_values(splits[0], (TOKENS, D), 1.0, 6.0, ((0, 64), (1, 8)))
    gate_weight = draw_gate_weight(jax.random.fold_in(splits[6], 71), 0)
    up_weight = draw_up_weight(jax.random.fold_in(splits[6], 71), 0)
    experts = draw_experts(jax.random.fold_in(splits[6], 71), 0)
    placement = draw_placement(jax.random.fold_in(splits[6], 71), 0)
    mix_weight = jnp.clip(0.1 + 0.9 * jax.random.uniform(splits[5], (TOKENS, TOP), jnp.float32) ** level_of(splits[5], (TOKENS, TOP), ((0, 64),), -0.2, 0.2), 0.1, 1.0)
    return dict(tokens=tokens, gate_weight=gate_weight, up_weight=up_weight, experts=experts, placement=placement, mix_weight=mix_weight)


def assign_slots(experts, placement):
    chosen_flat = experts.reshape(-1)
    expert_range = jnp.arange(EXPERTS, dtype=jnp.int32)
    holders = (placement[:, None] == expert_range[None, :]).astype(jnp.int32)
    replicas = jnp.sum(holders, axis=0)
    first_slot = jnp.sum((placement[:, None] < expert_range[None, :]).astype(jnp.int32), axis=0)
    chosen = (chosen_flat[:, None] == expert_range[None, :]).astype(jnp.int32)
    earlier = jnp.cumsum(chosen, axis=0) - chosen
    rank_index = jnp.sum(earlier * chosen, axis=1)
    replica_count = jnp.sum(chosen * replicas[None, :], axis=1)
    slot_start = jnp.sum(chosen * first_slot[None, :], axis=1)
    slot_index = slot_start + rank_index % replica_count
    position = rank_index // replica_count
    return slot_index.astype(jnp.int32), position.astype(jnp.int32)


def reference(tokens, gate_weight, up_weight, experts, placement, mix_weight):
    slot_index, position = jax.vmap(assign_slots, in_axes=(0, None))(experts.reshape(N_ED, TOK_DEV, TOP), placement)
    source_index = jnp.arange(N_ED, dtype=jnp.int32)[:, None]
    flat_place = ((slot_index * N_ED + source_index) * MOST + position).reshape(-1).astype(jnp.int32)
    pair_rows = jnp.repeat(tokens, TOP, axis=0)
    buffer = jnp.zeros((SLOTS * N_ED * MOST, D), jnp.bfloat16).at[flat_place].set(pair_rows)
    buffer = buffer.reshape(SLOTS, N_ED * MOST, D)
    gate_slots = gate_weight.reshape(SLOTS, GROUP, D, N_TP, FF_DEV)
    up_slots = up_weight.reshape(SLOTS, GROUP, D, N_TP, FF_DEV)

    def expert_block(operands):
        row_block, gate_part, up_part = operands
        gate_full = gate_part.transpose(1, 2, 0, 3).reshape(D, FF)
        up_full = up_part.transpose(1, 2, 0, 3).reshape(D, FF)
        gate_sum = jnp.dot(row_block, gate_full, preferred_element_type=jnp.float32)
        up_sum = jnp.dot(row_block, up_full, preferred_element_type=jnp.float32)
        return (jax.nn.silu(gate_sum) * up_sum).astype(jnp.bfloat16)

    hidden = lax.map(expert_block, (buffer, gate_slots, up_slots)).reshape(SLOTS * N_ED * MOST, FF)
    pair_hidden = hidden[flat_place]
    weighted = pair_hidden.astype(jnp.float32) * mix_weight.reshape(-1)[:, None]
    return weighted.astype(jnp.bfloat16).reshape(TOKENS, TOP, FF)
```

```python
import jax
import jax.numpy as jnp
from jax import lax
from jax.sharding import Mesh, PartitionSpec as P

EXPERTS = 8
MOST = 32
PLANE = ("xh", "core", "y", "xl")
ED = ("z", "xh", "core")


def assign_slots(experts, placement):
    chosen_flat = experts.reshape(-1)
    expert_range = jnp.arange(EXPERTS, dtype=jnp.int32)
    holders = (placement[:, None] == expert_range[None, :]).astype(jnp.int32)
    replicas = jnp.sum(holders, axis=0)
    first_slot = jnp.sum((placement[:, None] < expert_range[None, :]).astype(jnp.int32), axis=0)
    chosen = (chosen_flat[:, None] == expert_range[None, :]).astype(jnp.int32)
    earlier = jnp.cumsum(chosen, axis=0) - chosen
    rank_index = jnp.sum(earlier * chosen, axis=1)
    replica_count = jnp.sum(chosen * replicas[None, :], axis=1)
    slot_start = jnp.sum(chosen * first_slot[None, :], axis=1)
    slot_index = slot_start + rank_index % replica_count
    position = rank_index // replica_count
    return (slot_index, position)


def body(tokens, gate_weight, up_weight, experts, placement, mix_weight):
    tok_rows, width = tokens.shape
    top = experts.shape[1]
    slots = placement.shape[0]
    slot_index, position = assign_slots(experts, placement)
    place = slot_index * MOST + position
    spots = jnp.arange(slots * MOST, dtype=jnp.int32)
    pick = (place[:, None] == spots[None, :]).astype(jnp.bfloat16)
    spread = jnp.sum(pick.reshape(tok_rows, top, slots * MOST), axis=1)
    rows = lax.dot_general(
        spread, tokens, (((0,), (0,)), ((), ())), preferred_element_type=jnp.float32
    ).astype(jnp.bfloat16)
    arrived = lax.all_to_all(
        rows.reshape(slots, MOST, width), "z", split_axis=0, concat_axis=0, tiled=True
    ).reshape(slots * MOST, width)
    whole = lax.all_gather(arrived, PLANE, axis=0, tiled=False)
    whole = whole.reshape(4, 8, slots, MOST, width).transpose(2, 0, 3, 1, 4)
    whole = whole.reshape(slots * 4 * MOST, 8 * width)
    gate_sum = jnp.dot(whole, gate_weight[0], preferred_element_type=jnp.float32)
    up_sum = jnp.dot(whole, up_weight[0], preferred_element_type=jnp.float32)
    hidden = (jax.nn.silu(gate_sum) * up_sum).astype(jnp.bfloat16)
    units = hidden.shape[1]
    returned = lax.all_to_all(
        hidden.reshape(slots * 4, MOST, units), ED, split_axis=0, concat_axis=0, tiled=True
    )
    by_row = returned.reshape(slots, 4, MOST, units).transpose(0, 2, 1, 3)
    by_row = by_row.reshape(slots * MOST, 4 * units)
    pairs = jnp.dot(pick, by_row, preferred_element_type=jnp.float32)
    weighted = pairs * mix_weight.reshape(-1)[:, None]
    return weighted.astype(jnp.bfloat16).reshape(tok_rows, top, 4 * units)


def solution(mesh):
    fine = Mesh(mesh.devices.reshape(16, 2, 2, 4, 2), ("z", "xh", "core", "y", "xl"))
    tp = ("y", "xl")
    placed = (
        P(ED, tp),
        P(ED, None, tp),
        P(ED, None, tp),
        P(ED, None),
        P(),
        P(ED, None),
    )
    return jax.shard_map(
        body, mesh=fine, in_specs=placed, out_specs=P(ED, None, tp), check_vma=False
    )
```

```python
import jax
import jax.numpy as jnp
from jax import lax
from jax.experimental import pallas as pl
from jax.experimental.pallas import tpu as pltpu
from jax.sharding import Mesh, PartitionSpec as P

EXPERTS = 8
MOST = 32
SLOTS = 16
WIDTH = 384
UNITS = 256
ED = ("z", "xh", "core")
MESH = pl.DeviceIdType.MESH

PLAN = (
    ((0, 1), (-1, 8)),
    ((7, -6), (-7, 6)),
    ((5, -4), (-5, 4)),
    ((3, -2), (-3, 2)),
)
GROUPS = len(PLAN)
PER = 2
BLOCK = PER * MOST


def assign_slots(experts, placement):
    chosen_flat = experts.reshape(-1)
    expert_range = jnp.arange(EXPERTS, dtype=jnp.int32)
    holders = (placement[:, None] == expert_range[None, :]).astype(jnp.int32)
    replicas = jnp.sum(holders, axis=0)
    first_slot = jnp.sum((placement[:, None] < expert_range[None, :]).astype(jnp.int32), axis=0)
    chosen = (chosen_flat[:, None] == expert_range[None, :]).astype(jnp.int32)
    earlier = jnp.cumsum(chosen, axis=0) - chosen
    rank_index = jnp.sum(earlier * chosen, axis=1)
    replica_count = jnp.sum(chosen * replicas[None, :], axis=1)
    slot_start = jnp.sum(chosen * first_slot[None, :], axis=1)
    slot_index = slot_start + rank_index % replica_count
    position = rank_index // replica_count
    return (slot_index, position)


def kernel(
    rows, gate_hbm, up_hbm, pick, mix, out,
    full, gate_w, up_w, hidden, back,
    w_sem, z_send, z_recv, first_send, first_recv, second_send, second_recv,
    core_send, core_recv, back_send, back_recv,
):
    z, xh, core = lax.axis_index("z"), lax.axis_index("xh"), lax.axis_index("core")
    y, xl = lax.axis_index("y"), lax.axis_index("xl")
    x = xh * 2 + xl

    def x_at(step):
        other = lax.rem(x + step + 4, 4)
        return other // 2, lax.rem(other, 2)

    def y_at(step):
        return lax.rem(y + step + 4, 4)

    def z_at(step):
        return lax.rem(z + step + SLOTS, SLOTS)

    def x_device(step):
        other_h, other_l = x_at(step)
        return (z, other_h, core, y, other_l)

    def y_device(step):
        return (z, xh, core, y_at(step), xl)

    sibling = (z, xh, 1 - core, y, xl)

    def ed_device(dz, dh, dc):
        return (z_at(dz), 1 - xh if dh else xh, 1 - core if dc else core, y, xl)

    gate_copy = pltpu.make_async_copy(gate_hbm.at[0], gate_w, w_sem.at[0])
    up_copy = pltpu.make_async_copy(up_hbm.at[0], up_w, w_sem.at[1])
    gate_copy.start()
    up_copy.start()

    barrier = pltpu.get_barrier_semaphore()
    peers = 0
    for dz in range(SLOTS):
        for dh in range(2):
            for dc in range(2):
                if dz or dh or dc:
                    pl.semaphore_signal(
                        barrier, inc=1, device_id=ed_device(dz, dh, dc), device_id_type=MESH
                    )
                    peers += 1
    for step in (1, -1):
        pl.semaphore_signal(barrier, inc=1, device_id=x_device(step), device_id_type=MESH)
        pl.semaphore_signal(barrier, inc=1, device_id=y_device(step), device_id_type=MESH)
        peers += 2
    pl.semaphore_wait(barrier, peers)

    sends = []

    def remote(src, dst, send, recv, device):
        copy = pltpu.make_async_remote_copy(
            src_ref=src, dst_ref=dst, send_sem=send, recv_sem=recv,
            device_id=device, device_id_type=MESH,
        )
        copy.start()
        return copy

    def push(ref, send, recv, device):
        copy = remote(ref, ref, send, recv, device)
        sends.append(copy)

    def arrive(ref, recv):
        pltpu.make_async_copy(ref, ref, recv).wait()

    for g in range(GROUPS):
        for o in range(2):
            for j in range(PER):
                offset = PLAN[g][o][j]
                target = z_at(-offset)
                src = rows.at[pl.ds(pl.multiple_of(target * MOST, MOST), MOST)]
                dst = full.at[g, o, y, xl, xh, core, pl.ds(j * MOST, MOST)]
                if offset == 0:
                    pltpu.make_async_copy(src, dst, z_recv.at[g, o]).start()
                else:
                    remote(src, dst, z_send, z_recv.at[g, o], ed_device(-offset, 0, 0))

    def block(g, o, step):
        if o == 0:
            h, l = x_at(step)
            return full.at[g, o, y, l, h, core]
        return full.at[g, o, y_at(step), xl, xh, core]

    def half_block(g, o, step, half):
        part = pl.ds(half * (BLOCK // 2), BLOCK // 2)
        if o == 0:
            h, l = x_at(step)
            return full.at[g, o, y, l, h, core, part]
        return full.at[g, o, y_at(step), xl, xh, core, part]

    def slab(g, o, step):
        if o == 0:
            return full.at[g, o, y_at(step), :, :, core]
        h, l = x_at(step)
        return full.at[g, o, :, l, h, core]

    def half_slab(g, o, step, half):
        if o == 0:
            return full.at[g, o, y_at(step), half, :, core]
        h, l = x_at(step)
        return full.at[g, o, pl.ds(half * 2, 2), l, h, core]

    def first_device(o, step):
        return x_device(step) if o == 0 else y_device(step)

    def second_device(o, step):
        return y_device(step) if o == 0 else x_device(step)

    def to_core(g, o, ref):
        remote(ref, ref, core_send.at[g, o], core_recv.at[g, o], sibling)

    def stage0(g, o):
        arrive(block(g, o, 0), z_recv.at[g, o])
        for d, step in enumerate((1, -1)):
            push(block(g, o, 0), first_send.at[g, o, d], first_recv.at[g, o, d], first_device(o, step))

    def stage1(g, o):
        for d, step in enumerate((1, -1)):
            arrive(block(g, o, -step), first_recv.at[g, o, d])
            push(
                half_block(g, o, -step, d), first_send.at[g, o, 2 + d], first_recv.at[g, o, 2 + d],
                first_device(o, step),
            )

    def stage2(g, o):
        for d in range(2):
            arrive(half_block(g, o, 2, d), first_recv.at[g, o, 2 + d])
        for d, step in enumerate((1, -1)):
            push(slab(g, o, 0), second_send.at[g, o, d], second_recv.at[g, o, d], second_device(o, step))
        to_core(g, o, slab(g, o, 0))

    def stage3(g, o):
        for d, step in enumerate((1, -1)):
            arrive(slab(g, o, -step), second_recv.at[g, o, d])
            push(
                half_slab(g, o, -step, d), second_send.at[g, o, 2 + d], second_recv.at[g, o, 2 + d],
                second_device(o, step),
            )
            to_core(g, o, slab(g, o, -step))

    def stage4(g, o):
        for d in range(2):
            arrive(half_slab(g, o, 2, d), second_recv.at[g, o, 2 + d])
        to_core(g, o, slab(g, o, 2))

    def stage5(g, o):
        arrive(full.at[g, o, :, :, :, 1 - core], core_recv.at[g, o])
        left = jnp.concatenate(
            [full[g, o, t // 2, t % 2].reshape(4 * BLOCK, WIDTH) for t in range(8)], axis=1
        )
        gate_sum = jnp.dot(left, gate_w[...], preferred_element_type=jnp.float32)
        up_sum = jnp.dot(left, up_w[...], preferred_element_type=jnp.float32)
        units = gate_sum / (1.0 + jnp.exp(-gate_sum)) * up_sum
        hidden[g, o] = units.astype(jnp.bfloat16).reshape(2, 2, BLOCK, UNITS)
        for j in range(PER):
            offset = PLAN[g][o][j]
            for dh in range(2):
                for dc in range(2):
                    h = 1 - xh if dh else xh
                    c = 1 - core if dc else core
                    src = hidden.at[g, o, h, c, pl.ds(j * MOST, MOST)]
                    dst = back.at[xh * 2 + core, pl.ds(pl.multiple_of(z * MOST, MOST), MOST)]
                    if offset == 0 and not dh and not dc:
                        pltpu.make_async_copy(src, dst, back_recv).start()
                    else:
                        remote(src, dst, back_send.at[g, o], back_recv, ed_device(offset, dh, dc))

    stages = (stage0, stage1, stage2, stage3, stage4, stage5)
    for t in range(GROUPS + len(stages) - 1):
        if t == len(stages) - 1:
            gate_copy.wait()
            up_copy.wait()
        for s, stage in enumerate(stages):
            g = t - s
            if 0 <= g < GROUPS:
                for o in range(2):
                    stage(g, o)

    arrive(rows.at[pl.ds(0, (SLOTS - 1) * MOST)], z_send)
    for copy in sends:
        copy.wait_send()
    for g in range(GROUPS):
        for o in range(2):
            arrive(full.at[g, o, :, :, :, core], core_send.at[g, o])
            if 0 in PLAN[g][o]:
                arrive(hidden.at[g, o, 0], back_send.at[g, o])
                arrive(hidden.at[g, o, 1, 0], back_send.at[g, o])
                arrive(hidden.at[g, o, 1, 1, pl.ds(0, BLOCK - MOST)], back_send.at[g, o])
            else:
                arrive(hidden.at[g, o], back_send.at[g, o])
    arrive(back, back_recv)
    for g in range(4):
        pairs = jnp.dot(pick[...], back[g], preferred_element_type=jnp.float32)
        out[:, g * UNITS:(g + 1) * UNITS] = (pairs * mix[...]).astype(jnp.bfloat16)


def body(tokens, gate_weight, up_weight, experts, placement, mix_weight):
    tok_rows, width = tokens.shape
    top = experts.shape[1]
    slots = placement.shape[0]
    slot_index, position = assign_slots(experts, placement)
    place = slot_index * MOST + position
    spots = jnp.arange(slots * MOST, dtype=jnp.int32)
    pick = (place[:, None] == spots[None, :]).astype(jnp.bfloat16)
    spread = jnp.sum(pick.reshape(tok_rows, top, slots * MOST), axis=1)
    rows = lax.dot_general(
        spread, tokens, (((0,), (0,)), ((), ())), preferred_element_type=jnp.float32
    ).astype(jnp.bfloat16)
    vmem = pl.BlockSpec(memory_space=pltpu.VMEM)
    anywhere = pl.BlockSpec(memory_space=pl.ANY)
    dma = pltpu.SemaphoreType.DMA
    feature_count = gate_weight.shape[1]
    weighted = pl.pallas_call(
        kernel,
        out_shape=jax.ShapeDtypeStruct((tok_rows * top, 4 * UNITS), jnp.bfloat16),
        in_specs=[vmem, anywhere, anywhere, vmem, vmem],
        out_specs=vmem,
        scratch_shapes=[
            pltpu.VMEM((GROUPS, 2, 4, 2, 2, 2, BLOCK, WIDTH), jnp.bfloat16),
            pltpu.VMEM((feature_count, UNITS), jnp.bfloat16),
            pltpu.VMEM((feature_count, UNITS), jnp.bfloat16),
            pltpu.VMEM((GROUPS, 2, 2, 2, BLOCK, UNITS), jnp.bfloat16),
            pltpu.VMEM((4, slots * MOST, UNITS), jnp.bfloat16),
            dma((2,)),
            dma,
            dma((GROUPS, 2)),
            dma((GROUPS, 2, 4)),
            dma((GROUPS, 2, 4)),
            dma((GROUPS, 2, 4)),
            dma((GROUPS, 2, 4)),
            dma((GROUPS, 2)),
            dma((GROUPS, 2)),
            dma((GROUPS, 2)),
            dma,
        ],
        compiler_params=pltpu.CompilerParams(
            collective_id=0, has_side_effects=True, vmem_limit_bytes=48 * 1024 * 1024
        ),
        cost_estimate=pl.CostEstimate(
            flops=2 * 2048 * 3072 * 512, bytes_accessed=4 << 20, transcendentals=2048 * 256
        ),
    )(rows, gate_weight, up_weight, pick, mix_weight.reshape(-1)[:, None])
    return weighted.reshape(tok_rows, top, 4 * UNITS)


def solution(mesh):
    fine = Mesh(mesh.devices.reshape(16, 2, 2, 4, 2), ("z", "xh", "core", "y", "xl"))
    tp = ("y", "xl")
    placed = (
        P(ED, tp),
        P(ED, None, tp),
        P(ED, None, tp),
        P(ED, None),
        P(),
        P(ED, None),
    )
    return jax.shard_map(
        body, mesh=fine, in_specs=placed, out_specs=P(ED, None, tp), check_vma=False
    )
```

```python
import jax
import jax.numpy as jnp
from jax import lax
from jax.experimental import pallas as pl
from jax.experimental.pallas import tpu as pltpu
from jax.sharding import Mesh, PartitionSpec as P

MOST = 32
SLOTS = 16
WIDTH = 384
UNITS = 256
TOK = 128
EXPERT_ROWS = 16
ED = ("z", "xh", "core")
MESH = pl.DeviceIdType.MESH

PLAN = (
    ((7,), (-7,)),
    ((6,), (-6,)),
    ((8, -5), (5, 4)),
    ((-4, 3), (-3, 2)),
    ((-2, 1), (-1, 0)),
)
GROUPS = len(PLAN)
PER = tuple(len(orders[0]) for orders in PLAN)
START = tuple(sum(2 * per * MOST for per in PER[:g]) for g in range(GROUPS))
LAG = 1.5
WAVE = 2
ORDER = (2, 3, 4, 1, 0, 5)
LAST = len(ORDER) - 1
SCHEDULE = sorted(
    ((s, g) for g in range(GROUPS) for s in range(LAST + 1)),
    key=lambda item: (item[0] + LAG * item[1], ORDER.index(item[0])),
)


def place_rows(experts, placement):
    named = lax.broadcasted_iota(jnp.int32, (EXPERT_ROWS, TOK), 0)
    chosen = [experts[k:k + 1, :] == named for k in range(2)]
    counts = (chosen[0].astype(jnp.float32) + chosen[1].astype(jnp.float32)).astype(jnp.bfloat16)
    before = lax.broadcasted_iota(jnp.int32, (TOK, TOK), 0) < lax.broadcasted_iota(jnp.int32, (TOK, TOK), 1)
    earlier = jnp.dot(counts, before.astype(jnp.bfloat16), preferred_element_type=jnp.float32)
    expert_of_slot = lax.broadcasted_iota(jnp.int32, (EXPERT_ROWS, SLOTS), 0)
    replicas = jnp.sum((placement == expert_of_slot).astype(jnp.float32), axis=1, keepdims=True)
    first = jnp.sum((placement < expert_of_slot).astype(jnp.float32), axis=1, keepdims=True)
    found = []
    for k in range(2):
        own = chosen[k].astype(jnp.float32)
        rank = jnp.sum(own * earlier, axis=0, keepdims=True)
        replica_count = jnp.sum(own * replicas, axis=0, keepdims=True)
        start = jnp.sum(own * first, axis=0, keepdims=True)
        position = jnp.floor((rank + 0.5) / replica_count)
        found.append((start + rank - position * replica_count, position))
    return found


def spread_rows(found):
    spot = lax.broadcasted_iota(jnp.int32, (SLOTS * MOST, TOK), 0).astype(jnp.float32)
    hits = [(slot * MOST + position == spot).astype(jnp.float32) for slot, position in found]
    return (hits[0] + hits[1]).astype(jnp.bfloat16)


def pick_rows(found, mix):
    lines = [found[0][0], found[1][0], found[0][1], found[1][1]]
    rest = mix
    for part in range(3):
        piece = rest.astype(jnp.bfloat16).astype(jnp.float32)
        rest = rest - piece
        lines += [piece[0:1, :], piece[1:2, :]]
    table = jnp.concatenate(lines + [jnp.zeros((EXPERT_ROWS - len(lines), TOK), jnp.float32)], axis=0)
    pair = lax.broadcasted_iota(jnp.int32, (2 * TOK, TOK), 0)
    token = lax.broadcasted_iota(jnp.int32, (2 * TOK, TOK), 1)
    mine = jnp.logical_or(pair == 2 * token, pair == 2 * token + 1)
    per_pair = lax.dot_general(
        mine.astype(jnp.bfloat16), table.astype(jnp.bfloat16), (((1,), (1,)), ((), ())),
        preferred_element_type=jnp.float32,
    )
    second = jnp.bitwise_and(lax.broadcasted_iota(jnp.int32, (2 * TOK, 1), 0), 1) == 1
    values = [jnp.where(second, per_pair[:, 2 * v + 1:2 * v + 2], per_pair[:, 2 * v:2 * v + 1]) for v in range(5)]
    spot = lax.broadcasted_iota(jnp.int32, (2 * TOK, SLOTS * MOST), 1).astype(jnp.float32)
    pick = (values[0] * MOST + values[1] == spot).astype(jnp.float32).astype(jnp.bfloat16)
    return pick, (values[2] + values[3]) + values[4]


def kernel(
    tokens_hbm, gate_hbm, up_hbm, experts_hbm, placement_hbm, mix_hbm, out,
    tokens, experts, placement, mix, rows, pick, scale, full, gate_w, up_w, hidden, back,
    w_sem, z_send, z_recv, first_send, first_recv, second_send, second_recv,
    core_send, core_recv, back_send, back_recv,
):
    z, xh, core = lax.axis_index("z"), lax.axis_index("xh"), lax.axis_index("core")
    y, xl = lax.axis_index("y"), lax.axis_index("xl")
    x = xh * 2 + xl

    def x_at(step):
        other = lax.rem(x + step + 4, 4)
        return other // 2, lax.rem(other, 2)

    def y_at(step):
        return lax.rem(y + step + 4, 4)

    def z_at(step):
        return lax.rem(z + step + SLOTS, SLOTS)

    def x_device(step):
        other_h, other_l = x_at(step)
        return (z, other_h, core, y, other_l)

    def y_device(step):
        return (z, xh, core, y_at(step), xl)

    sibling = (z, xh, 1 - core, y, xl)

    def ed_device(dz, dh, dc):
        return (z_at(dz), 1 - xh if dh else xh, 1 - core if dc else core, y, xl)

    barrier = pltpu.get_barrier_semaphore()
    peers = [ed_device(dz, 0, 0) for dz in range(1, SLOTS)] + [sibling]
    peers += [device(step) for device in (x_device, y_device) for step in (1, -1)]
    for peer in peers:
        pl.semaphore_signal(barrier, inc=1, device_id=peer, device_id_type=MESH)

    loads = [
        pltpu.make_async_copy(src, dst, w_sem.at[i])
        for i, (src, dst) in enumerate((
            (experts_hbm, experts), (placement_hbm, placement), (tokens_hbm, tokens),
            (mix_hbm, mix), (gate_hbm.at[0], gate_w), (up_hbm.at[0], up_w),
        ))
    ]
    for load in loads:
        load.start()
    loads[0].wait()
    loads[1].wait()
    found = place_rows(experts[...], placement[...])
    loads[2].wait()
    rows[...] = jnp.dot(
        spread_rows(found), tokens[...], preferred_element_type=jnp.float32
    ).astype(jnp.bfloat16)

    pl.semaphore_wait(barrier, len(peers))

    sends = []

    def remote(src, dst, send, recv, device):
        copy = pltpu.make_async_remote_copy(
            src_ref=src, dst_ref=dst, send_sem=send, recv_sem=recv,
            device_id=device, device_id_type=MESH,
        )
        copy.start()
        return copy

    def push(ref, send, recv, device):
        copy = remote(ref, ref, send, recv, device)
        sends.append(copy)

    def arrive(ref, recv):
        pltpu.make_async_copy(ref, ref, recv).wait()

    def send_rows(g):
        for o in range(2):
            for j, offset in enumerate(PLAN[g][o]):
                src = rows.at[pl.ds(pl.multiple_of(z_at(-offset) * MOST, MOST), MOST)]
                dst = full.at[y, xl, xh, core, pl.ds(begin(g, o) + j * MOST, MOST)]
                if offset == 0:
                    pltpu.make_async_copy(src, dst, z_recv.at[g, o]).start()
                else:
                    remote(src, dst, z_send, z_recv.at[g, o], ed_device(-offset, 0, 0))

    def begin(g, o):
        return START[g] + o * PER[g] * MOST

    def span(g, o):
        return pl.ds(begin(g, o), PER[g] * MOST)

    def block(g, o, step):
        if o == 0:
            h, l = x_at(step)
            return full.at[y, l, h, core, span(g, o)]
        return full.at[y_at(step), xl, xh, core, span(g, o)]

    def half_block(g, o, step, half):
        size = PER[g] * MOST // 2
        part = pl.ds(begin(g, o) + half * size, size)
        if o == 0:
            h, l = x_at(step)
            return full.at[y, l, h, core, part]
        return full.at[y_at(step), xl, xh, core, part]

    def slab(g, o, step):
        if o == 0:
            return full.at[y_at(step), :, :, core, span(g, o)]
        h, l = x_at(step)
        return full.at[:, l, h, core, span(g, o)]

    def half_slab(g, o, step, half):
        if o == 0:
            return full.at[y_at(step), half, :, core, span(g, o)]
        h, l = x_at(step)
        return full.at[pl.ds(half * 2, 2), l, h, core, span(g, o)]

    def first_device(o, step):
        return x_device(step) if o == 0 else y_device(step)

    def second_device(o, step):
        return y_device(step) if o == 0 else x_device(step)

    def to_core(g, o, ref):
        remote(ref, ref, core_send.at[g, o], core_recv.at[g, o], sibling)

    def stage0(g, o):
        arrive(block(g, o, 0), z_recv.at[g, o])
        for d, step in enumerate((1, -1)):
            push(block(g, o, 0), first_send.at[g, o, d], first_recv.at[g, o, d], first_device(o, step))

    def stage1(g, o):
        for d, step in enumerate((1, -1)):
            arrive(block(g, o, -step), first_recv.at[g, o, d])
            push(
                half_block(g, o, -step, d), first_send.at[g, o, 2 + d], first_recv.at[g, o, 2 + d],
                first_device(o, step),
            )

    def stage2(g, o):
        for d in range(2):
            arrive(half_block(g, o, 2, d), first_recv.at[g, o, 2 + d])
        for d, step in enumerate((1, -1)):
            push(slab(g, o, 0), second_send.at[g, o, d], second_recv.at[g, o, d], second_device(o, step))
        to_core(g, o, slab(g, o, 0))

    def stage3(g, o):
        for d, step in enumerate((1, -1)):
            arrive(slab(g, o, -step), second_recv.at[g, o, d])
            push(
                half_slab(g, o, -step, d), second_send.at[g, o, 2 + d], second_recv.at[g, o, 2 + d],
                second_device(o, step),
            )
            to_core(g, o, slab(g, o, -step))

    def stage4(g, o):
        for d in range(2):
            arrive(half_slab(g, o, 2, d), second_recv.at[g, o, 2 + d])
        to_core(g, o, slab(g, o, 2))

    def stage5(g):
        for o in range(2):
            arrive(full.at[:, :, :, 1 - core, span(g, o)], core_recv.at[g, o])
        count = 2 * PER[g] * MOST
        both = pl.ds(START[g], count)
        left = jnp.concatenate(
            [full[t // 2, t % 2, :, :, both, :].reshape(4 * count, WIDTH) for t in range(8)], axis=1
        )
        gate_sum = jnp.dot(left, gate_w[...], preferred_element_type=jnp.float32)
        up_sum = jnp.dot(left, up_w[...], preferred_element_type=jnp.float32)
        units = gate_sum / (1.0 + jnp.exp(-gate_sum)) * up_sum
        hidden[:, :, both, :] = units.astype(jnp.bfloat16).reshape(2, 2, count, UNITS)
        for o in range(2):
            for j, offset in enumerate(PLAN[g][o]):
                for dh in range(2):
                    for dc in range(2):
                        h = 1 - xh if dh else xh
                        c = 1 - core if dc else core
                        src = hidden.at[h, c, pl.ds(begin(g, o) + j * MOST, MOST)]
                        dst = back.at[xh * 2 + core, pl.ds(pl.multiple_of(z * MOST, MOST), MOST)]
                        if offset == 0 and not dh and not dc:
                            pltpu.make_async_copy(src, dst, back_recv).start()
                        else:
                            remote(src, dst, back_send.at[g], back_recv, ed_device(offset, dh, dc))

    for g in range(WAVE):
        send_rows(g)
    loads[3].wait()
    found_pick, found_scale = pick_rows(found, mix[...])
    pick[...] = found_pick
    scale[...] = found_scale
    stages = (stage0, stage1, stage2, stage3, stage4)
    for s, g in SCHEDULE:
        if s == LAST:
            if g == 0:
                loads[4].wait()
                loads[5].wait()
            stage5(g)
            continue
        for o in range(2):
            stages[s](g, o)
        if s == 0 and g + WAVE < GROUPS:
            send_rows(g + WAVE)

    arrive(rows.at[pl.ds(0, (SLOTS - 1) * MOST)], z_send)
    for copy in sends:
        copy.wait_send()
    for g in range(GROUPS):
        for o in range(2):
            arrive(full.at[:, :, :, core, span(g, o)], core_send.at[g, o])
        count = 2 * PER[g] * MOST
        if 0 in PLAN[g][0] + PLAN[g][1]:
            arrive(hidden.at[0, :, pl.ds(START[g], count)], back_send.at[g])
            arrive(hidden.at[1, 0, pl.ds(START[g], count)], back_send.at[g])
            arrive(hidden.at[1, 1, pl.ds(START[g], count - MOST)], back_send.at[g])
        else:
            arrive(hidden.at[:, :, pl.ds(START[g], count)], back_send.at[g])
    arrive(back, back_recv)
    for g in range(4):
        pairs = jnp.dot(pick[...], back[g], preferred_element_type=jnp.float32)
        out[:, g * UNITS:(g + 1) * UNITS] = (pairs * scale[...]).astype(jnp.bfloat16)


def body(tokens, gate_weight, up_weight, experts, placement, mix_weight):
    tok_rows, width = tokens.shape
    top = experts.shape[1]
    slots = placement.shape[0]
    vmem = pl.BlockSpec(memory_space=pltpu.VMEM)
    hbm = pl.BlockSpec(memory_space=pltpu.HBM)
    dma = pltpu.SemaphoreType.DMA
    feature_count = gate_weight.shape[1]
    weighted = pl.pallas_call(
        kernel,
        out_shape=jax.ShapeDtypeStruct((tok_rows * top, 4 * UNITS), jnp.bfloat16),
        in_specs=[hbm] * 6,
        out_specs=vmem,
        scratch_shapes=[
            pltpu.VMEM((tok_rows, width), jnp.bfloat16),
            pltpu.VMEM((top, tok_rows), jnp.int32),
            pltpu.VMEM((1, slots), jnp.int32),
            pltpu.VMEM((top, tok_rows), jnp.float32),
            pltpu.VMEM((slots * MOST, width), jnp.bfloat16),
            pltpu.VMEM((tok_rows * top, slots * MOST), jnp.bfloat16),
            pltpu.VMEM((tok_rows * top, 1), jnp.float32),
            pltpu.VMEM((4, 2, 2, 2, slots * MOST, width), jnp.bfloat16),
            pltpu.VMEM((feature_count, UNITS), jnp.bfloat16),
            pltpu.VMEM((feature_count, UNITS), jnp.bfloat16),
            pltpu.VMEM((2, 2, slots * MOST, UNITS), jnp.bfloat16),
            pltpu.VMEM((4, slots * MOST, UNITS), jnp.bfloat16),
            dma((6,)),
            dma,
            dma((GROUPS, 2)),
            dma((GROUPS, 2, 4)),
            dma((GROUPS, 2, 4)),
            dma((GROUPS, 2, 4)),
            dma((GROUPS, 2, 4)),
            dma((GROUPS, 2)),
            dma((GROUPS, 2)),
            dma((GROUPS,)),
            dma,
        ],
        compiler_params=pltpu.CompilerParams(
            collective_id=0, has_side_effects=True, vmem_limit_bytes=60 * 1024 * 1024
        ),
        cost_estimate=pl.CostEstimate(
            flops=2 * 2048 * 3072 * 512, bytes_accessed=4 << 20, transcendentals=2048 * 256
        ),
    )(tokens, gate_weight, up_weight, experts.T, placement.reshape(1, slots), mix_weight.T)
    return weighted.reshape(tok_rows, top, 4 * UNITS)


def solution(mesh):
    fine = Mesh(mesh.devices.reshape(16, 2, 2, 4, 2), ("z", "xh", "core", "y", "xl"))
    tp = ("y", "xl")
    placed = (
        P(ED, tp),
        P(ED, None, tp),
        P(ED, None, tp),
        P(ED, None),
        P(),
        P(ED, None),
    )
    return jax.shard_map(
        body, mesh=fine, in_specs=placed, out_specs=P(ED, None, tp), check_vma=False
    )
```

```python
import jax
import jax.numpy as jnp
from jax import lax
from jax.experimental import pallas as pl
from jax.experimental.pallas import tpu as pltpu
from jax.sharding import Mesh, PartitionSpec as P

MOST = 32
SLOTS = 16
WIDTH = 384
UNITS = 256
TOK = 128
EXPERT_ROWS = 16
ED = ("z", "xh", "core")
MESH = pl.DeviceIdType.MESH

PLAN = (
    ((5,), (-5,)),
    ((7,), (-7,)),
    ((6,), (-6,)),
    ((8, -4), (4, 3)),
    ((-3, 2), (-2, 0)),
    ((1,), (-1,)),
)
GROUPS = len(PLAN)
PER = tuple(len(orders[0]) for orders in PLAN)
DIRECT = 6
START = tuple(sum(2 * per * MOST for per in PER[:g]) for g in range(GROUPS))
ROWS, RETURN = -1, 5
SCHEDULE = (
    (-1, 2, 0), (-1, 1, 0), (-1, 3, 0), (0, 2, 1), (0, 2, 0), (-1, 5, 0), (0, 1, 0), (0, 1, 1),
    (1, 2, 1), (2, 2, 1), (1, 2, 0), (2, 2, 0), (-1, 0, 0), (0, 3, 0), (1, 1, 1), (1, 1, 0),
    (-1, 4, 0), (0, 3, 1), (2, 1, 1), (0, 5, 1), (2, 1, 0), (3, 2, 1), (4, 2, 1), (0, 5, 0),
    (3, 2, 0), (4, 2, 0), (1, 3, 1), (1, 3, 0), (2, 3, 0), (2, 3, 1), (5, 2, 0), (0, 0, 0),
    (3, 1, 0), (3, 1, 1), (1, 5, 1), (4, 1, 1), (4, 1, 0), (0, 4, 0), (1, 5, 0), (0, 0, 1),
    (2, 5, 1), (0, 4, 1), (5, 1, 0), (3, 3, 1), (2, 5, 0), (3, 3, 0), (4, 3, 1), (4, 3, 0),
    (1, 0, 1), (2, 0, 1), (1, 0, 0), (1, 4, 1), (1, 4, 0), (2, 0, 0), (2, 4, 1), (2, 4, 0),
    (5, 3, 0), (3, 5, 0), (3, 5, 1), (4, 5, 1), (3, 0, 1), (3, 0, 0), (4, 0, 0), (4, 0, 1),
    (4, 5, 0), (3, 4, 0), (5, 0, 0), (3, 4, 1), (4, 4, 0), (4, 4, 1), (5, 5, 0), (5, 4, 0),
)


def place_rows(experts, placement):
    named = lax.broadcasted_iota(jnp.int32, (EXPERT_ROWS, TOK), 0)
    chosen = [experts[k:k + 1, :] == named for k in range(2)]
    counts = (chosen[0].astype(jnp.float32) + chosen[1].astype(jnp.float32)).astype(jnp.bfloat16)
    before = lax.broadcasted_iota(jnp.int32, (TOK, TOK), 0) < lax.broadcasted_iota(jnp.int32, (TOK, TOK), 1)
    earlier = jnp.dot(counts, before.astype(jnp.bfloat16), preferred_element_type=jnp.float32)
    expert_of_slot = lax.broadcasted_iota(jnp.int32, (EXPERT_ROWS, SLOTS), 0)
    replicas = jnp.sum((placement == expert_of_slot).astype(jnp.float32), axis=1, keepdims=True)
    first = jnp.sum((placement < expert_of_slot).astype(jnp.float32), axis=1, keepdims=True)
    found = []
    for k in range(2):
        own = chosen[k].astype(jnp.float32)
        rank = jnp.sum(own * earlier, axis=0, keepdims=True)
        replica_count = jnp.sum(own * replicas, axis=0, keepdims=True)
        start = jnp.sum(own * first, axis=0, keepdims=True)
        position = jnp.floor((rank + 0.5) / replica_count)
        found.append((start + rank - position * replica_count, position))
    return found


def spread_rows(found):
    spot = lax.broadcasted_iota(jnp.int32, (SLOTS * MOST, TOK), 0).astype(jnp.float32)
    hits = [(slot * MOST + position == spot).astype(jnp.float32) for slot, position in found]
    return (hits[0] + hits[1]).astype(jnp.bfloat16)


def pick_rows(found, mix):
    lines = [found[0][0], found[1][0], found[0][1], found[1][1]]
    rest = mix
    for part in range(3):
        piece = rest.astype(jnp.bfloat16).astype(jnp.float32)
        rest = rest - piece
        lines += [piece[0:1, :], piece[1:2, :]]
    table = jnp.concatenate(lines + [jnp.zeros((EXPERT_ROWS - len(lines), TOK), jnp.float32)], axis=0)
    pair = lax.broadcasted_iota(jnp.int32, (2 * TOK, TOK), 0)
    token = lax.broadcasted_iota(jnp.int32, (2 * TOK, TOK), 1)
    mine = jnp.logical_or(pair == 2 * token, pair == 2 * token + 1)
    per_pair = lax.dot_general(
        mine.astype(jnp.bfloat16), table.astype(jnp.bfloat16), (((1,), (1,)), ((), ())),
        preferred_element_type=jnp.float32,
    )
    second = jnp.bitwise_and(lax.broadcasted_iota(jnp.int32, (2 * TOK, 1), 0), 1) == 1
    values = [jnp.where(second, per_pair[:, 2 * v + 1:2 * v + 2], per_pair[:, 2 * v:2 * v + 1]) for v in range(5)]
    spot = lax.broadcasted_iota(jnp.int32, (2 * TOK, SLOTS * MOST), 1).astype(jnp.float32)
    pick = (values[0] * MOST + values[1] == spot).astype(jnp.float32).astype(jnp.bfloat16)
    return pick, (values[2] + values[3]) + values[4]


def kernel(
    tokens_hbm, gate_hbm, up_hbm, experts_hbm, placement_hbm, mix_hbm, out,
    tokens, experts, placement, mix, rows, pick, scale, full, gate_w, up_w, hidden, back,
    w_sem, z_send, z_recv, first_send, first_recv, second_send, second_recv,
    core_send, core_recv, back_send, back_recv,
):
    z, xh, core = lax.axis_index("z"), lax.axis_index("xh"), lax.axis_index("core")
    y, xl = lax.axis_index("y"), lax.axis_index("xl")
    x = xh * 2 + xl

    def x_at(step):
        other = lax.rem(x + step + 4, 4)
        return other // 2, lax.rem(other, 2)

    def y_at(step):
        return lax.rem(y + step + 4, 4)

    def z_at(step):
        return lax.rem(z + step + SLOTS, SLOTS)

    def x_device(step):
        other_h, other_l = x_at(step)
        return (z, other_h, core, y, other_l)

    def y_device(step):
        return (z, xh, core, y_at(step), xl)

    sibling = (z, xh, 1 - core, y, xl)

    def ed_device(dz, dh, dc):
        return (z_at(dz), 1 - xh if dh else xh, 1 - core if dc else core, y, xl)

    barrier = pltpu.get_barrier_semaphore()
    peers = [ed_device(dz, 0, 0) for dz in range(1, SLOTS)] + [sibling]
    peers += [device(step) for device in (x_device, y_device) for step in (1, -1, 2)]
    for peer in peers:
        pl.semaphore_signal(barrier, inc=1, device_id=peer, device_id_type=MESH)

    loads = [
        pltpu.make_async_copy(src, dst, w_sem.at[i])
        for i, (src, dst) in enumerate((
            (experts_hbm, experts), (placement_hbm, placement), (tokens_hbm, tokens),
            (mix_hbm, mix), (gate_hbm.at[0], gate_w), (up_hbm.at[0], up_w),
        ))
    ]
    for load in loads:
        load.start()
    loads[0].wait()
    loads[1].wait()
    found = place_rows(experts[...], placement[...])
    loads[2].wait()
    rows[...] = jnp.dot(
        spread_rows(found), tokens[...], preferred_element_type=jnp.float32
    ).astype(jnp.bfloat16)

    pl.semaphore_wait(barrier, len(peers))

    sends = []

    def remote(src, dst, send, recv, device):
        copy = pltpu.make_async_remote_copy(
            src_ref=src, dst_ref=dst, send_sem=send, recv_sem=recv,
            device_id=device, device_id_type=MESH,
        )
        copy.start()
        return copy

    def push(ref, send, recv, device):
        copy = remote(ref, ref, send, recv, device)
        sends.append(copy)

    def arrive(ref, recv):
        pltpu.make_async_copy(ref, ref, recv).wait()

    def send_rows(g):
        for o in range(2):
            for j, offset in enumerate(PLAN[g][o]):
                src = rows.at[pl.ds(pl.multiple_of(z_at(-offset) * MOST, MOST), MOST)]
                dst = full.at[y, xl, xh, core, pl.ds(begin(g, o) + j * MOST, MOST)]
                if offset == 0:
                    pltpu.make_async_copy(src, dst, z_recv.at[g, o]).start()
                else:
                    remote(src, dst, z_send, z_recv.at[g, o], ed_device(-offset, 0, 0))

    def begin(g, o):
        return START[g] + o * PER[g] * MOST

    def span(g, o):
        return pl.ds(begin(g, o), PER[g] * MOST)

    def block(g, o, step):
        if o == 0:
            h, l = x_at(step)
            return full.at[y, l, h, core, span(g, o)]
        return full.at[y_at(step), xl, xh, core, span(g, o)]

    def half_block(g, o, step, half):
        size = PER[g] * MOST // 2
        part = pl.ds(begin(g, o) + half * size, size)
        if o == 0:
            h, l = x_at(step)
            return full.at[y, l, h, core, part]
        return full.at[y_at(step), xl, xh, core, part]

    def slab(g, o, step):
        if o == 0:
            return full.at[y_at(step), :, :, core, span(g, o)]
        h, l = x_at(step)
        return full.at[:, l, h, core, span(g, o)]

    def half_slab(g, o, step, half):
        if o == 0:
            return full.at[y_at(step), half, :, core, span(g, o)]
        h, l = x_at(step)
        return full.at[pl.ds(half * 2, 2), l, h, core, span(g, o)]

    def first_device(o, step):
        return x_device(step) if o == 0 else y_device(step)

    def second_device(o, step):
        return y_device(step) if o == 0 else x_device(step)

    def to_core(g, o, ref):
        remote(ref, ref, core_send.at[g, o], core_recv.at[g, o], sibling)

    def ways(g):
        return (1, -1, 2) if g < DIRECT else (1, -1)

    def stage0(g, o):
        arrive(block(g, o, 0), z_recv.at[g, o])
        for d, step in enumerate(ways(g)):
            push(block(g, o, 0), first_send.at[g, o, d], first_recv.at[g, o, d], first_device(o, step))

    def stage1(g, o):
        for d, step in enumerate((1, -1)):
            arrive(block(g, o, -step), first_recv.at[g, o, d])
            if g >= DIRECT:
                push(
                    half_block(g, o, -step, d), first_send.at[g, o, 2 + d], first_recv.at[g, o, 2 + d],
                    first_device(o, step),
                )

    def stage2(g, o):
        if g < DIRECT:
            arrive(block(g, o, 2), first_recv.at[g, o, 2])
        else:
            for d in range(2):
                arrive(half_block(g, o, 2, d), first_recv.at[g, o, 2 + d])
        for d, step in enumerate(ways(g)):
            push(slab(g, o, 0), second_send.at[g, o, d], second_recv.at[g, o, d], second_device(o, step))
        to_core(g, o, slab(g, o, 0))

    def stage3(g, o):
        for d, step in enumerate((1, -1)):
            arrive(slab(g, o, -step), second_recv.at[g, o, d])
            if g >= DIRECT:
                push(
                    half_slab(g, o, -step, d), second_send.at[g, o, 2 + d], second_recv.at[g, o, 2 + d],
                    second_device(o, step),
                )
            to_core(g, o, slab(g, o, -step))

    def stage4(g, o):
        if g < DIRECT:
            arrive(slab(g, o, 2), second_recv.at[g, o, 2])
        else:
            for d in range(2):
                arrive(half_slab(g, o, 2, d), second_recv.at[g, o, 2 + d])
        to_core(g, o, slab(g, o, 2))

    def stage5(g):
        for o in range(2):
            arrive(full.at[:, :, :, 1 - core, span(g, o)], core_recv.at[g, o])
        count = 2 * PER[g] * MOST
        both = pl.ds(START[g], count)
        left = jnp.concatenate(
            [full[t // 2, t % 2, :, :, both, :].reshape(4 * count, WIDTH) for t in range(8)], axis=1
        )
        gate_sum = jnp.dot(left, gate_w[...], preferred_element_type=jnp.float32)
        up_sum = jnp.dot(left, up_w[...], preferred_element_type=jnp.float32)
        units = gate_sum / (1.0 + jnp.exp(-gate_sum)) * up_sum
        hidden[:, :, both, :] = units.astype(jnp.bfloat16).reshape(2, 2, count, UNITS)
        for o in range(2):
            for j, offset in enumerate(PLAN[g][o]):
                for dh in range(2):
                    for dc in range(2):
                        h = 1 - xh if dh else xh
                        c = 1 - core if dc else core
                        src = hidden.at[h, c, pl.ds(begin(g, o) + j * MOST, MOST)]
                        dst = back.at[xh * 2 + core, pl.ds(pl.multiple_of(z * MOST, MOST), MOST)]
                        if offset == 0 and not dh and not dc:
                            pltpu.make_async_copy(src, dst, back_recv).start()
                        else:
                            remote(src, dst, back_send.at[g], back_recv, ed_device(offset, dh, dc))

    def before_return():
        loads[3].wait()
        found_pick, found_scale = pick_rows(found, mix[...])
        pick[...] = found_pick
        scale[...] = found_scale
        loads[4].wait()
        loads[5].wait()

    stages = (stage0, stage1, stage2, stage3, stage4)
    returning = False
    for s, g, o in SCHEDULE:
        if s == ROWS:
            send_rows(g)
        elif s == RETURN:
            if not returning:
                before_return()
                returning = True
            stage5(g)
        else:
            stages[s](g, o)

    arrive(rows.at[pl.ds(0, (SLOTS - 1) * MOST)], z_send)
    for copy in sends:
        copy.wait_send()
    for g in range(GROUPS):
        for o in range(2):
            arrive(full.at[:, :, :, core, span(g, o)], core_send.at[g, o])
        count = 2 * PER[g] * MOST
        if 0 in PLAN[g][0] + PLAN[g][1]:
            arrive(hidden.at[0, :, pl.ds(START[g], count)], back_send.at[g])
            arrive(hidden.at[1, 0, pl.ds(START[g], count)], back_send.at[g])
            arrive(hidden.at[1, 1, pl.ds(START[g], count - MOST)], back_send.at[g])
        else:
            arrive(hidden.at[:, :, pl.ds(START[g], count)], back_send.at[g])
    arrive(back, back_recv)
    for g in range(4):
        pairs = jnp.dot(pick[...], back[g], preferred_element_type=jnp.float32)
        out[:, g * UNITS:(g + 1) * UNITS] = (pairs * scale[...]).astype(jnp.bfloat16)


def body(tokens, gate_weight, up_weight, experts, placement, mix_weight):
    tok_rows, width = tokens.shape
    top = experts.shape[1]
    slots = placement.shape[0]
    vmem = pl.BlockSpec(memory_space=pltpu.VMEM)
    hbm = pl.BlockSpec(memory_space=pltpu.HBM)
    dma = pltpu.SemaphoreType.DMA
    feature_count = gate_weight.shape[1]
    weighted = pl.pallas_call(
        kernel,
        out_shape=jax.ShapeDtypeStruct((tok_rows * top, 4 * UNITS), jnp.bfloat16),
        in_specs=[hbm] * 6,
        out_specs=vmem,
        scratch_shapes=[
            pltpu.VMEM((tok_rows, width), jnp.bfloat16),
            pltpu.VMEM((top, tok_rows), jnp.int32),
            pltpu.VMEM((1, slots), jnp.int32),
            pltpu.VMEM((top, tok_rows), jnp.float32),
            pltpu.VMEM((slots * MOST, width), jnp.bfloat16),
            pltpu.VMEM((tok_rows * top, slots * MOST), jnp.bfloat16),
            pltpu.VMEM((tok_rows * top, 1), jnp.float32),
            pltpu.VMEM((4, 2, 2, 2, slots * MOST, width), jnp.bfloat16),
            pltpu.VMEM((feature_count, UNITS), jnp.bfloat16),
            pltpu.VMEM((feature_count, UNITS), jnp.bfloat16),
            pltpu.VMEM((2, 2, slots * MOST, UNITS), jnp.bfloat16),
            pltpu.VMEM((4, slots * MOST, UNITS), jnp.bfloat16),
            dma((6,)),
            dma,
            dma((GROUPS, 2)),
            dma((GROUPS, 2, 4)),
            dma((GROUPS, 2, 4)),
            dma((GROUPS, 2, 4)),
            dma((GROUPS, 2, 4)),
            dma((GROUPS, 2)),
            dma((GROUPS, 2)),
            dma((GROUPS,)),
            dma,
        ],
        compiler_params=pltpu.CompilerParams(
            collective_id=0, has_side_effects=True, vmem_limit_bytes=60 * 1024 * 1024
        ),
        cost_estimate=pl.CostEstimate(
            flops=2 * 2048 * 3072 * 512, bytes_accessed=4 << 20, transcendentals=2048 * 256
        ),
    )(tokens, gate_weight, up_weight, experts.T, placement.reshape(1, slots), mix_weight.T)
    return weighted.reshape(tok_rows, top, 4 * UNITS)


def solution(mesh):
    fine = Mesh(mesh.devices.reshape(16, 2, 2, 4, 2), ("z", "xh", "core", "y", "xl"))
    tp = ("y", "xl")
    placed = (
        P(ED, tp),
        P(ED, None, tp),
        P(ED, None, tp),
        P(ED, None),
        P(),
        P(ED, None),
    )
    return jax.shard_map(
        body, mesh=fine, in_specs=placed, out_specs=P(ED, None, tp), check_vma=False
    )
```

```python
import jax
import jax.numpy as jnp
from jax import lax
from jax.experimental import pallas as pl
from jax.experimental.pallas import tpu as pltpu
from jax.sharding import Mesh, PartitionSpec as P

MOST = 32
SLOTS = 16
WIDTH = 384
UNITS = 256
TOK = 128
EXPERT_ROWS = 16
ED = ("z", "xh", "core")
MESH = pl.DeviceIdType.MESH

PLAN = (
    ((5,), (-5,)),
    ((7,), (-7,)),
    ((6,), (-6,)),
    ((8, -4), (4, 3)),
    ((-3, 2), (-2, 0)),
    ((1,), (-1,)),
)
GROUPS = len(PLAN)
PER = tuple(len(orders[0]) for orders in PLAN)
DIRECT = 6
START = tuple(sum(2 * per * MOST for per in PER[:g]) for g in range(GROUPS))
ROWS, RETURN = -1, 5
SCHEDULE = (
    (-1, 2, 0), (-1, 1, 0), (-1, 3, 0), (0, 2, 1), (0, 2, 0), (-1, 5, 0), (0, 1, 0), (0, 1, 1),
    (1, 2, 1), (2, 2, 1), (1, 2, 0), (2, 2, 0), (-1, 0, 0), (0, 3, 0), (1, 1, 1), (1, 1, 0),
    (-1, 4, 0), (0, 3, 1), (2, 1, 1), (0, 5, 1), (2, 1, 0), (3, 2, 1), (4, 2, 1), (0, 5, 0),
    (3, 2, 0), (4, 2, 0), (1, 3, 1), (1, 3, 0), (2, 3, 0), (2, 3, 1), (5, 2, 0), (0, 0, 0),
    (3, 1, 0), (3, 1, 1), (1, 5, 1), (4, 1, 1), (4, 1, 0), (0, 4, 0), (1, 5, 0), (0, 0, 1),
    (2, 5, 1), (0, 4, 1), (5, 1, 0), (3, 3, 1), (2, 5, 0), (3, 3, 0), (4, 3, 1), (4, 3, 0),
    (1, 0, 1), (2, 0, 1), (1, 0, 0), (1, 4, 1), (1, 4, 0), (2, 0, 0), (2, 4, 1), (2, 4, 0),
    (5, 3, 0), (3, 5, 0), (3, 5, 1), (4, 5, 1), (3, 0, 1), (3, 0, 0), (4, 0, 0), (4, 0, 1),
    (4, 5, 0), (3, 4, 0), (5, 0, 0), (3, 4, 1), (4, 4, 0), (4, 4, 1), (5, 5, 0), (5, 4, 0),
)


def place_rows(experts, placement):
    named = lax.broadcasted_iota(jnp.int32, (EXPERT_ROWS, TOK), 0)
    chosen = [experts[k:k + 1, :] == named for k in range(2)]
    counts = (chosen[0].astype(jnp.float32) + chosen[1].astype(jnp.float32)).astype(jnp.bfloat16)
    before = lax.broadcasted_iota(jnp.int32, (TOK, TOK), 0) < lax.broadcasted_iota(jnp.int32, (TOK, TOK), 1)
    earlier = jnp.dot(counts, before.astype(jnp.bfloat16), preferred_element_type=jnp.float32)
    expert_of_slot = lax.broadcasted_iota(jnp.int32, (EXPERT_ROWS, SLOTS), 0)
    replicas = jnp.sum((placement == expert_of_slot).astype(jnp.float32), axis=1, keepdims=True)
    first = jnp.sum((placement < expert_of_slot).astype(jnp.float32), axis=1, keepdims=True)
    found = []
    for k in range(2):
        own = chosen[k].astype(jnp.float32)
        rank = jnp.sum(own * earlier, axis=0, keepdims=True)
        replica_count = jnp.sum(own * replicas, axis=0, keepdims=True)
        start = jnp.sum(own * first, axis=0, keepdims=True)
        position = jnp.floor((rank + 0.5) / replica_count)
        found.append((start + rank - position * replica_count, position))
    return found


def spread_rows(found):
    spot = lax.broadcasted_iota(jnp.int32, (SLOTS * MOST, TOK), 0).astype(jnp.float32)
    hits = [(slot * MOST + position == spot).astype(jnp.float32) for slot, position in found]
    return (hits[0] + hits[1]).astype(jnp.bfloat16)


def pick_rows(found, mix):
    lines = [found[0][0], found[1][0], found[0][1], found[1][1]]
    rest = mix
    for part in range(3):
        piece = rest.astype(jnp.bfloat16).astype(jnp.float32)
        rest = rest - piece
        lines += [piece[0:1, :], piece[1:2, :]]
    table = jnp.concatenate(lines + [jnp.zeros((EXPERT_ROWS - len(lines), TOK), jnp.float32)], axis=0)
    pair = lax.broadcasted_iota(jnp.int32, (2 * TOK, TOK), 0)
    token = lax.broadcasted_iota(jnp.int32, (2 * TOK, TOK), 1)
    mine = jnp.logical_or(pair == 2 * token, pair == 2 * token + 1)
    per_pair = lax.dot_general(
        mine.astype(jnp.bfloat16), table.astype(jnp.bfloat16), (((1,), (1,)), ((), ())),
        preferred_element_type=jnp.float32,
    )
    second = jnp.bitwise_and(lax.broadcasted_iota(jnp.int32, (2 * TOK, 1), 0), 1) == 1
    values = [jnp.where(second, per_pair[:, 2 * v + 1:2 * v + 2], per_pair[:, 2 * v:2 * v + 1]) for v in range(5)]
    spot = lax.broadcasted_iota(jnp.int32, (2 * TOK, SLOTS * MOST), 1).astype(jnp.float32)
    pick = (values[0] * MOST + values[1] == spot).astype(jnp.float32).astype(jnp.bfloat16)
    return pick, (values[2] + values[3]) + values[4]


def kernel(
    tokens_hbm, gate_hbm, up_hbm, experts_hbm, placement_hbm, mix_hbm, out,
    tokens, experts, placement, mix, rows, pick, scale, full, gate_w, up_w, hidden, back,
    w_sem, z_send, z_recv, first_send, first_recv, second_send, second_recv,
    core_send, core_recv, back_send, back_recv,
):
    z, xh, core = lax.axis_index("z"), lax.axis_index("xh"), lax.axis_index("core")
    y, xl = lax.axis_index("y"), lax.axis_index("xl")
    x = xh * 2 + xl

    def x_at(step):
        other = lax.rem(x + step + 4, 4)
        return other // 2, lax.rem(other, 2)

    def y_at(step):
        return lax.rem(y + step + 4, 4)

    def z_at(step):
        return lax.rem(z + step + SLOTS, SLOTS)

    def x_device(step):
        other_h, other_l = x_at(step)
        return (z, other_h, core, y, other_l)

    def y_device(step):
        return (z, xh, core, y_at(step), xl)

    sibling = (z, xh, 1 - core, y, xl)

    def ed_device(dz, dh, dc):
        return (z_at(dz), 1 - xh if dh else xh, 1 - core if dc else core, y, xl)

    barrier = pltpu.get_barrier_semaphore()
    peers = [ed_device(dz, 0, 0) for dz in range(1, SLOTS)] + [sibling]
    peers += [device(step) for device in (x_device, y_device) for step in (1, -1, 2)]
    for peer in peers:
        pl.semaphore_signal(barrier, inc=1, device_id=peer, device_id_type=MESH)

    loads = [
        pltpu.make_async_copy(src, dst, w_sem.at[i])
        for i, (src, dst) in enumerate((
            (experts_hbm, experts), (placement_hbm, placement), (tokens_hbm, tokens),
            (mix_hbm, mix), (gate_hbm.at[0], gate_w), (up_hbm.at[0], up_w),
        ))
    ]
    for load in loads:
        load.start()
    loads[0].wait()
    loads[1].wait()
    found = place_rows(experts[...], placement[...])
    loads[2].wait()
    rows[...] = jnp.dot(
        spread_rows(found), tokens[...], preferred_element_type=jnp.float32
    ).astype(jnp.bfloat16)

    pl.semaphore_wait(barrier, len(peers))

    sends = []

    def remote(src, dst, send, recv, device):
        copy = pltpu.make_async_remote_copy(
            src_ref=src, dst_ref=dst, send_sem=send, recv_sem=recv,
            device_id=device, device_id_type=MESH,
        )
        copy.start()
        return copy

    def push(ref, send, recv, device):
        copy = remote(ref, ref, send, recv, device)
        sends.append(copy)

    def arrive(ref, recv):
        pltpu.make_async_copy(ref, ref, recv).wait()

    def send_rows(g):
        for o in range(2):
            for j, offset in enumerate(PLAN[g][o]):
                src = rows.at[pl.ds(pl.multiple_of(z_at(-offset) * MOST, MOST), MOST)]
                dst = full.at[y, xl, xh, core, pl.ds(begin(g, o) + j * MOST, MOST)]
                if offset == 0:
                    pltpu.make_async_copy(src, dst, z_recv.at[g, o]).start()
                else:
                    remote(src, dst, z_send, z_recv.at[g, o], ed_device(-offset, 0, 0))

    def begin(g, o):
        return START[g] + o * PER[g] * MOST

    def span(g, o):
        return pl.ds(begin(g, o), PER[g] * MOST)

    def block(g, o, step):
        if o == 0:
            h, l = x_at(step)
            return full.at[y, l, h, core, span(g, o)]
        return full.at[y_at(step), xl, xh, core, span(g, o)]

    def half_block(g, o, step, half):
        size = PER[g] * MOST // 2
        part = pl.ds(begin(g, o) + half * size, size)
        if o == 0:
            h, l = x_at(step)
            return full.at[y, l, h, core, part]
        return full.at[y_at(step), xl, xh, core, part]

    def slab(g, o, step):
        if o == 0:
            return full.at[y_at(step), :, :, core, span(g, o)]
        h, l = x_at(step)
        return full.at[:, l, h, core, span(g, o)]

    def half_slab(g, o, step, half):
        if o == 0:
            return full.at[y_at(step), half, :, core, span(g, o)]
        h, l = x_at(step)
        return full.at[pl.ds(half * 2, 2), l, h, core, span(g, o)]

    def first_device(o, step):
        return x_device(step) if o == 0 else y_device(step)

    def second_device(o, step):
        return y_device(step) if o == 0 else x_device(step)

    def to_core(g, o, ref):
        remote(ref, ref, core_send.at[g, o], core_recv.at[g, o], sibling)

    def ways(g):
        return (1, -1, 2) if g < DIRECT else (1, -1)

    def stage0(g, o):
        arrive(block(g, o, 0), z_recv.at[g, o])
        for d, step in enumerate(ways(g)):
            push(block(g, o, 0), first_send.at[g, o, d], first_recv.at[g, o, d], first_device(o, step))

    def stage1(g, o):
        for d, step in enumerate((1, -1)):
            arrive(block(g, o, -step), first_recv.at[g, o, d])
            if g >= DIRECT:
                push(
                    half_block(g, o, -step, d), first_send.at[g, o, 2 + d], first_recv.at[g, o, 2 + d],
                    first_device(o, step),
                )

    def stage2(g, o):
        if g < DIRECT:
            arrive(block(g, o, 2), first_recv.at[g, o, 2])
        else:
            for d in range(2):
                arrive(half_block(g, o, 2, d), first_recv.at[g, o, 2 + d])
        for d, step in enumerate(ways(g)):
            push(slab(g, o, 0), second_send.at[g, o, d], second_recv.at[g, o, d], second_device(o, step))
        to_core(g, o, slab(g, o, 0))

    def stage3(g, o):
        for d, step in enumerate((1, -1)):
            arrive(slab(g, o, -step), second_recv.at[g, o, d])
            if g >= DIRECT:
                push(
                    half_slab(g, o, -step, d), second_send.at[g, o, 2 + d], second_recv.at[g, o, 2 + d],
                    second_device(o, step),
                )
            to_core(g, o, slab(g, o, -step))

    def stage4(g, o):
        if g < DIRECT:
            arrive(slab(g, o, 2), second_recv.at[g, o, 2])
        else:
            for d in range(2):
                arrive(half_slab(g, o, 2, d), second_recv.at[g, o, 2 + d])
        to_core(g, o, slab(g, o, 2))

    def stage5(g):
        for o in range(2):
            arrive(full.at[:, :, :, 1 - core, span(g, o)], core_recv.at[g, o])
        count = 2 * PER[g] * MOST
        both = pl.ds(START[g], count)
        left = jnp.concatenate(
            [full[t // 2, t % 2, :, :, both, :].reshape(4 * count, WIDTH) for t in range(8)], axis=1
        )
        gate_sum = jnp.dot(left, gate_w[...], preferred_element_type=jnp.float32)
        up_sum = jnp.dot(left, up_w[...], preferred_element_type=jnp.float32)
        units = gate_sum / (1.0 + jnp.exp(-gate_sum)) * up_sum
        hidden[:, :, both, :] = units.astype(jnp.bfloat16).reshape(2, 2, count, UNITS)
        for o in range(2):
            for j, offset in enumerate(PLAN[g][o]):
                for dh in range(2):
                    for dc in range(2):
                        h = 1 - xh if dh else xh
                        c = 1 - core if dc else core
                        src = hidden.at[h, c, pl.ds(begin(g, o) + j * MOST, MOST)]
                        dst = back.at[xh * 2 + core, pl.ds(pl.multiple_of(z * MOST, MOST), MOST)]
                        if offset == 0 and not dh and not dc:
                            pltpu.make_async_copy(src, dst, back_recv).start()
                        else:
                            remote(src, dst, back_send.at[g], back_recv, ed_device(offset, dh, dc))

    def before_return():
        loads[4].wait()
        loads[5].wait()

    stages = (stage0, stage1, stage2, stage3, stage4)
    returning = False
    for s, g, o in SCHEDULE:
        if s == ROWS:
            send_rows(g)
        elif s == RETURN:
            if not returning:
                before_return()
                returning = True
            stage5(g)
        else:
            stages[s](g, o)

    loads[3].wait()
    found_pick, found_scale = pick_rows(found, mix[...])
    pick[...] = found_pick
    scale[...] = found_scale

    arrive(rows.at[pl.ds(0, (SLOTS - 1) * MOST)], z_send)
    for copy in sends:
        copy.wait_send()
    for g in range(GROUPS):
        for o in range(2):
            arrive(full.at[:, :, :, core, span(g, o)], core_send.at[g, o])
        count = 2 * PER[g] * MOST
        if 0 in PLAN[g][0] + PLAN[g][1]:
            arrive(hidden.at[0, :, pl.ds(START[g], count)], back_send.at[g])
            arrive(hidden.at[1, 0, pl.ds(START[g], count)], back_send.at[g])
            arrive(hidden.at[1, 1, pl.ds(START[g], count - MOST)], back_send.at[g])
        else:
            arrive(hidden.at[:, :, pl.ds(START[g], count)], back_send.at[g])
    arrive(back, back_recv)
    for g in range(4):
        pairs = jnp.dot(pick[...], back[g], preferred_element_type=jnp.float32)
        out[:, g * UNITS:(g + 1) * UNITS] = (pairs * scale[...]).astype(jnp.bfloat16)


def body(tokens, gate_weight, up_weight, experts, placement, mix_weight):
    tok_rows, width = tokens.shape
    top = experts.shape[1]
    slots = placement.shape[0]
    vmem = pl.BlockSpec(memory_space=pltpu.VMEM)
    hbm = pl.BlockSpec(memory_space=pltpu.HBM)
    dma = pltpu.SemaphoreType.DMA
    feature_count = gate_weight.shape[1]
    weighted = pl.pallas_call(
        kernel,
        out_shape=jax.ShapeDtypeStruct((tok_rows * top, 4 * UNITS), jnp.bfloat16),
        in_specs=[hbm] * 6,
        out_specs=vmem,
        scratch_shapes=[
            pltpu.VMEM((tok_rows, width), jnp.bfloat16),
            pltpu.VMEM((top, tok_rows), jnp.int32),
            pltpu.VMEM((1, slots), jnp.int32),
            pltpu.VMEM((top, tok_rows), jnp.float32),
            pltpu.VMEM((slots * MOST, width), jnp.bfloat16),
            pltpu.VMEM((tok_rows * top, slots * MOST), jnp.bfloat16),
            pltpu.VMEM((tok_rows * top, 1), jnp.float32),
            pltpu.VMEM((4, 2, 2, 2, slots * MOST, width), jnp.bfloat16),
            pltpu.VMEM((feature_count, UNITS), jnp.bfloat16),
            pltpu.VMEM((feature_count, UNITS), jnp.bfloat16),
            pltpu.VMEM((2, 2, slots * MOST, UNITS), jnp.bfloat16),
            pltpu.VMEM((4, slots * MOST, UNITS), jnp.bfloat16),
            dma((6,)),
            dma,
            dma((GROUPS, 2)),
            dma((GROUPS, 2, 4)),
            dma((GROUPS, 2, 4)),
            dma((GROUPS, 2, 4)),
            dma((GROUPS, 2, 4)),
            dma((GROUPS, 2)),
            dma((GROUPS, 2)),
            dma((GROUPS,)),
            dma,
        ],
        compiler_params=pltpu.CompilerParams(
            collective_id=0, has_side_effects=True, vmem_limit_bytes=60 * 1024 * 1024
        ),
        cost_estimate=pl.CostEstimate(
            flops=2 * 2048 * 3072 * 512, bytes_accessed=4 << 20, transcendentals=2048 * 256
        ),
    )(tokens, gate_weight, up_weight, experts.T, placement.reshape(1, slots), mix_weight.T)
    return weighted.reshape(tok_rows, top, 4 * UNITS)


def solution(mesh):
    fine = Mesh(mesh.devices.reshape(16, 2, 2, 4, 2), ("z", "xh", "core", "y", "xl"))
    tp = ("y", "xl")
    placed = (
        P(ED, tp),
        P(ED, None, tp),
        P(ED, None, tp),
        P(ED, None),
        P(),
        P(ED, None),
    )
    return jax.shard_map(
        body, mesh=fine, in_specs=placed, out_specs=P(ED, None, tp), check_vma=False
    )
```
